32 devices in a mesh: tiles: 8 (over z, y), chan: 4 (over x, core).
Axes of the slice: x: 2, y: 2, z: 4, core: 2. Of those that a mesh axis runs over, the one named last changes fastest.
Arguments:
- x_scan: bfloat16 [128, 192, 256], P('tiles', 'chan'), may hold values from -40 to 40
- slot_owner: int32 [128], P('tiles'), may hold values from 0 to 64, as said below
- adjacency: int32 [64, 8], P('tiles'), may hold values from 0 to 64, as said below
- cotangent: bfloat16 [64, 192, 256], P('tiles', 'chan'), may hold values from -6 to 6
- dw_weight: float32 [192, 49], P('chan'), may hold values from -0.875 to 0.875
- ln_gain: bfloat16 [192], P('chan'), may hold values from 0.25 to 1.75
- w_in: bfloat16 [192, 768], P(None, 'chan'), may hold values from -0.4375 to 0.4375
- b_in: bfloat16 [768], P('chan'), may hold values from -3 to 3
- w_out: bfloat16 [768, 192], P('chan'), may hold values from -0.21875 to 0.21875
- layer_scale: float32 [192], P('chan'), may hold values from 0.3 to 1.5
Outputs:
- output: bfloat16 [64, 192, 256], P('tiles', 'chan')
- grad_in: bfloat16 [64, 192, 256], P('tiles', 'chan')
- grad_dw: float32 [192, 49], P('chan')
- grad_w1: float32 [192, 768], P(None, 'chan')
- grad_w2: float32 [768, 192], P('chan')
The draws below stay inside these ranges and needn't reach their ends.
Inputs may be any that keep to these rules, and one draw needn't show every extreme that they name: `slot_owner`: slots run in scan order over a grid of tiles with 16 columns, one grid row for each device along tiles. A tissue slot holds its tile's owner-order index, a background slot holds 64. Tissue tiles are numbered in scan order, and owner-order index q belongs to device q // 8. Grid rows 2k and 2k + 1 hold 4 to 12 tissue tiles each and 16 together, so a device's tissue tiles belong to it or to the device whose index differs in the lowest bit, and at most 4 of them, a number reached in every draw, to the latter. `adjacency`: entry k of a tissue tile is the owner-order index of the grid cell at row and column offsets (-1,-1), (-1,0), (-1,1), (0,-1), (0,1), (1,-1), (1,0), (1,1) from it, 64 where that cell is background or off the grid. Every neighbour of a tile owned by device o is owned by one of the devices o - 3 to o + 3, a distance reached in every draw.
All inputs are finite; a program needn't handle non-finite values.
Results may differ from the reference program's by a relative error of at most 0.015.
Values may be sent and summed in bfloat16 or wider, within the bound.
A program may use at most 128 MiB of HBM per device.

```python
import math
import jax
import jax.numpy as jnp
from jax import lax

CHANNEL_COUNT = 192
HID = 768
P_SIZE = 16
TILE_DEV = 8
PIX = 256
HID_DEV = 192
TILES = 64
SLOTS = 128


def tissue_layout(key):
    grid_rows = TILES // TILE_DEV
    grid_cols = 2 * TILE_DEV
    half_dev = TILE_DEV // 2
    pair_count = grid_rows // 2
    offsets = jax.random.randint(jax.random.fold_in(key, 1), (pair_count,), -half_dev, half_dev + 1)
    offsets = offsets.at[0].set(-half_dev).at[1].set(half_dev)
    counts = jnp.stack([TILE_DEV + offsets, TILE_DEV - offsets], axis=1).reshape(grid_rows)
    row_keys = jax.random.split(jax.random.fold_in(key, 2), grid_rows)

    def shuffled(row_key):
        return jax.random.permutation(row_key, grid_cols)
    orders = jax.vmap(shuffled)(row_keys)
    tissue = orders < counts[:, None]
    column_ids = jnp.arange(grid_cols)
    tissue = tissue.at[1].set(column_ids >= half_dev).at[2].set(column_ids < grid_cols - half_dev)
    flags = tissue.reshape(-1).astype(jnp.int32)
    ranks = jnp.cumsum(flags) - flags
    owners = jnp.where(flags > 0, ranks, TILES).astype(jnp.int32)
    owner_grid = jnp.pad(owners.reshape(grid_rows, grid_cols), 1, constant_values=TILES)
    neighbours = []
    for row_step in (-1, 0, 1):
        for col_step in (-1, 0, 1):
            if row_step != 0 or col_step != 0:
                neighbours.append(owner_grid[1 + row_step:1 + row_step + grid_rows, 1 + col_step:1 + col_step + grid_cols].reshape(-1))
    neighbour_table = jnp.stack(neighbours, axis=1).astype(jnp.int32)
    adjacency = jnp.full((TILES, 8), TILES, jnp.int32).at[owners].set(neighbour_table, mode='drop')
    return (owners, adjacency)


def draw_slot_owner(key, part):
    return tissue_layout(jax.random.fold_in(key, 5))[0]


def draw_adjacency(key, part):
    return tissue_layout(jax.random.fold_in(key, 5))[1]


def draw_x_scan(key, part):
    value_key = jax.random.fold_in(key, 11)
    chan_key = jax.random.fold_in(key, 12)
    tile_key = jax.random.fold_in(key, 13)
    chan_scale = jnp.exp(jax.random.uniform(chan_key, (CHANNEL_COUNT,), jnp.float32, math.log(0.3), math.log(3.0)))
    tile_scale = jnp.exp(jax.random.uniform(tile_key, (SLOTS, 1, 1), jnp.float32, math.log(0.5), math.log(2.0)))
    values = jax.random.truncated_normal(value_key, -4.0, 4.0, (SLOTS, CHANNEL_COUNT, PIX), jnp.float32)
    return (values * chan_scale[None, :, None] * tile_scale).astype(jnp.bfloat16)


def block_scale(stream_key, dims, pieces, low, largest):
    def one(position, blocks):
        steps = jax.random.uniform(jax.random.fold_in(jax.random.fold_in(stream_key, 6), position), (blocks,), jnp.float32, low / len(pieces), largest / len(pieces))
        return jnp.repeat(jnp.exp(steps), dims[position] // blocks).reshape((-1,) + (1,) * (len(dims) - position - 1))

    factor_of = one(*pieces[0])
    for cut in pieces[1:]:
        factor_of = factor_of * one(*cut)
    return factor_of


def scatter_about(key, extent, scale, reach, shards=(), kind=jnp.bfloat16):
    drawn = scale * jax.random.normal(key, extent, jnp.float32)
    if shards:
        drawn = drawn * block_scale(key, extent, shards, -0.22, 0.18)
    return jnp.clip(drawn, -reach, reach).astype(kind)


def setup_inputs(seed: int = 0) -> dict:
    seeds = jax.random.split(jax.random.key(seed), 11)
    return {
        "x_scan": draw_x_scan(jax.random.fold_in(seeds[10], 71), 0),
        "slot_owner": draw_slot_owner(jax.random.fold_in(seeds[10], 71), 0),
        "adjacency": draw_adjacency(jax.random.fold_in(seeds[10], 71), 0),
        "cotangent": scatter_about(seeds[3], (TILES, CHANNEL_COUNT, PIX), 1.0, 6.0, ((0, 8), (1, 4))),
        "dw_weight": scatter_about(seeds[4], (CHANNEL_COUNT, 49), 49 ** -0.5, 0.875, ((0, 4),), jnp.float32),
        "ln_gain": jnp.clip(1.0 + 0.15 * jax.random.normal(seeds[5], (CHANNEL_COUNT,), jnp.float32), 0.25, 1.75).astype(jnp.bfloat16),
        "w_in": scatter_about(seeds[6], (CHANNEL_COUNT, HID), CHANNEL_COUNT ** -0.5, 0.4375, ((1, 4),)),
        "b_in": scatter_about(seeds[7], (HID,), 0.5, 3.0, ((0, 4),)),
        "w_out": scatter_about(seeds[8], (HID, CHANNEL_COUNT), HID ** -0.5, 0.21875, ((0, 4),)),
        "layer_scale": jnp.clip(jnp.exp(math.log(1.5) - 1.60943787 * jax.random.uniform(seeds[9], (CHANNEL_COUNT,), jnp.float32) ** block_scale(seeds[9], (CHANNEL_COUNT,), ((0, 4),), -0.2, 0.2)), 0.3, 1.5),
    }


EPSILON = 1e-06
GELU_SCALE = 0.7978845608
GELU_CUBIC = 0.044715

def strips(tile_field):
    side_len = tile_field.shape[-1]
    top_rows = tile_field[:, :, :3, :]
    bottom_rows = tile_field[:, :, side_len - 3:, :]
    left_cols = jnp.swapaxes(tile_field[:, :, :, :3], 2, 3)
    right_cols = jnp.swapaxes(tile_field[:, :, :, side_len - 3:], 2, 3)
    return jnp.stack([top_rows, bottom_rows, left_cols, right_cols], axis=2)

def assemble(tile_field, around):
    side_len = tile_field.shape[-1]
    upper_band = jnp.concatenate([around[:, 0, :, 1, :, side_len - 3:], around[:, 1, :, 1], around[:, 2, :, 1, :, :3]], axis=3)
    middle = jnp.concatenate([jnp.swapaxes(around[:, 3, :, 3], 2, 3), tile_field, jnp.swapaxes(around[:, 4, :, 2], 2, 3)], axis=3)
    lower_band = jnp.concatenate([around[:, 5, :, 0, :, side_len - 3:], around[:, 6, :, 0], around[:, 7, :, 0, :, :3]], axis=3)
    return jnp.concatenate([upper_band, middle, lower_band], axis=2)

def depthwise(padded, kernel):
    tile_count = padded.shape[0]
    channels = padded.shape[1]
    wide_len = padded.shape[3]
    side_len = wide_len - 6
    span_len = side_len * wide_len
    flat_pad = jnp.pad(padded.astype(jnp.float32).reshape(tile_count, channels, wide_len * wide_len), ((0, 0), (0, 0), (0, 8)))
    result = jnp.zeros((tile_count, channels, span_len), jnp.float32)
    for row_tap in range(7):
        for col_tap in range(7):
            offset = row_tap * wide_len + col_tap
            result = result + kernel[:, row_tap * 7 + col_tap][None, :, None] * flat_pad[:, :, offset:offset + span_len]
    return result.reshape(tile_count, channels, side_len, wide_len)[:, :, :, :side_len]

def kernel_grad(grad_tiles, padded):
    tile_count = grad_tiles.shape[0]
    channels = grad_tiles.shape[1]
    side_len = grad_tiles.shape[3]
    wide_len = side_len + 6
    span_len = side_len * wide_len
    flat_pad = jnp.pad(padded.astype(jnp.float32).reshape(tile_count, channels, wide_len * wide_len), ((0, 0), (0, 0), (0, 8)))
    spread = jnp.pad(grad_tiles.astype(jnp.float32), ((0, 0), (0, 0), (0, 0), (0, 6))).reshape(tile_count, channels, span_len)
    columns = []
    for row_tap in range(7):
        for col_tap in range(7):
            offset = row_tap * wide_len + col_tap
            columns.append(lax.optimization_barrier(jnp.sum(spread * flat_pad[:, :, offset:offset + span_len], axis=(0, 2))))
    return jnp.stack(columns, axis=1)

def gelu_parts(preact):
    tanh_arg = GELU_SCALE * (preact + GELU_CUBIC * preact * preact * preact)
    tangent = jnp.tanh(tanh_arg)
    values = 0.5 * preact * (1.0 + tangent)
    slopes = 0.5 * (1.0 + tangent) + 0.5 * preact * (1.0 - tangent * tangent) * GELU_SCALE * (1.0 + 3.0 * GELU_CUBIC * preact * preact)
    return (values, slopes)

def lookup(rim_table, neighbours):
    return jnp.take(rim_table, neighbours, axis=0, mode='fill', fill_value=0)

def reference(x_scan, slot_owner, adjacency, cotangent, dw_weight, ln_gain, w_in, b_in, w_out, layer_scale):
    owned_tiles = jnp.zeros((TILES, CHANNEL_COUNT, PIX), jnp.bfloat16).at[slot_owner].set(x_scan, mode='drop')
    tile_field = owned_tiles.reshape(TILES, CHANNEL_COUNT, P_SIZE, P_SIZE)
    rim_table = strips(tile_field)
    gain_float = ln_gain.astype(jnp.float32)
    bias_f = b_in.astype(jnp.float32)
    w_in_f = w_in.astype(jnp.float32)
    w_out_f = w_out.astype(jnp.float32)
    groups = HID // HID_DEV
    scale_col = layer_scale[None, :, None]
    block_ids = jnp.arange(TILES // TILE_DEV, dtype=jnp.int32)

    def forward_block(carry, block_id):
        start = (block_id * TILE_DEV).astype(jnp.int32)
        field_block = lax.dynamic_slice_in_dim(tile_field, start, TILE_DEV, 0)
        adj_block = lax.dynamic_slice_in_dim(adjacency, start, TILE_DEV, 0)
        cot_block = lax.dynamic_slice_in_dim(cotangent, start, TILE_DEV, 0)
        padded = assemble(field_block, lookup(rim_table, adj_block))
        mixed_tiles = depthwise(padded, dw_weight).astype(jnp.bfloat16).reshape(TILE_DEV, CHANNEL_COUNT, PIX)
        mixed_f = mixed_tiles.astype(jnp.float32)
        row_mean = lax.optimization_barrier(jnp.sum(mixed_f, axis=1)) / CHANNEL_COUNT
        inverse_deviation = lax.rsqrt(lax.optimization_barrier(jnp.sum(mixed_f * mixed_f, axis=1)) / CHANNEL_COUNT - row_mean * row_mean + EPSILON)
        centered_input = (mixed_f - row_mean[:, None, :]) * inverse_deviation[:, None, :]
        normed = (centered_input * gain_float[None, :, None]).astype(jnp.bfloat16)
        preact = jnp.einsum('tcp,ch->thp', normed.astype(jnp.float32), w_in_f) + bias_f[None, :, None]
        values, slopes = gelu_parts(preact)
        activated = values.astype(jnp.bfloat16)
        branch_parts = jnp.einsum('tqhp,qhc->tqcp', activated.astype(jnp.float32).reshape(TILE_DEV, groups, HID_DEV, PIX), w_out_f.reshape(groups, HID_DEV, CHANNEL_COUNT))
        branch = lax.optimization_barrier(jnp.sum(lax.optimization_barrier(branch_parts.astype(jnp.bfloat16)).astype(jnp.float32), axis=1)).astype(jnp.bfloat16)
        field_flat = field_block.reshape(TILE_DEV, CHANNEL_COUNT, PIX)
        output = (field_flat.astype(jnp.float32) + scale_col * branch.astype(jnp.float32)).astype(jnp.bfloat16)
        dbranch = (cot_block.astype(jnp.float32) * scale_col).astype(jnp.bfloat16)
        act_grad = jnp.einsum('tcp,hc->thp', dbranch.astype(jnp.float32), w_out_f)
        pre_grad = (act_grad * slopes).astype(jnp.bfloat16)
        part_w2 = jnp.einsum('thp,tcp->hc', activated.astype(jnp.float32), dbranch.astype(jnp.float32))
        part_w1 = jnp.einsum('tcp,thp->ch', normed.astype(jnp.float32), pre_grad.astype(jnp.float32))
        input_parts = jnp.einsum('tqhp,cqh->tqcp', pre_grad.astype(jnp.float32).reshape(TILE_DEV, groups, HID_DEV, PIX), w_in_f.reshape(CHANNEL_COUNT, groups, HID_DEV))
        normed_gradient = lax.optimization_barrier(jnp.sum(lax.optimization_barrier(input_parts.astype(jnp.bfloat16)).astype(jnp.float32), axis=1))
        centered_input_gradient = normed_gradient * gain_float[None, :, None]
        mean_first_moment = lax.optimization_barrier(jnp.sum(centered_input_gradient, axis=1)) / CHANNEL_COUNT
        mean_second_moment = lax.optimization_barrier(jnp.sum(centered_input_gradient * centered_input, axis=1)) / CHANNEL_COUNT
        mixed_gradient = (inverse_deviation[:, None, :] * (centered_input_gradient - mean_first_moment[:, None, :] - centered_input * mean_second_moment[:, None, :])).astype(jnp.bfloat16)
        return ((carry[0] + part_w1, carry[1] + part_w2), (output, mixed_gradient))
    start_sums = (jnp.zeros((CHANNEL_COUNT, HID), jnp.float32), jnp.zeros((HID, CHANNEL_COUNT), jnp.float32))
    raw_sums, stacked = lax.scan(forward_block, start_sums, block_ids)
    output = stacked[0].reshape(TILES, CHANNEL_COUNT, PIX)
    grad_field = stacked[1].reshape(TILES, CHANNEL_COUNT, P_SIZE, P_SIZE)
    grad_rims = strips(grad_field)

    def backward_block(carry, block_id):
        start = (block_id * TILE_DEV).astype(jnp.int32)
        field_block = lax.dynamic_slice_in_dim(tile_field, start, TILE_DEV, 0)
        grad_block = lax.dynamic_slice_in_dim(grad_field, start, TILE_DEV, 0)
        adj_block = lax.dynamic_slice_in_dim(adjacency, start, TILE_DEV, 0)
        cot_block = lax.dynamic_slice_in_dim(cotangent, start, TILE_DEV, 0)
        padded = assemble(field_block, lookup(rim_table, adj_block))
        dpadded = assemble(grad_block, lookup(grad_rims, adj_block))
        backflow = depthwise(dpadded, dw_weight[:, ::-1]).reshape(TILE_DEV, CHANNEL_COUNT, PIX)
        grad_in = (cot_block.astype(jnp.float32) + backflow).astype(jnp.bfloat16)
        return (carry + kernel_grad(grad_block, padded), grad_in)
    raw_dw, grad_blocks = lax.scan(backward_block, jnp.zeros((CHANNEL_COUNT, 49), jnp.float32), block_ids)
    factor = 1.0 / math.sqrt(TILES * PIX)
    return (output, grad_blocks.reshape(TILES, CHANNEL_COUNT, PIX), raw_dw * factor, raw_sums[0] * factor, raw_sums[1] * factor)
```

```python
import math

import jax
import jax.numpy as jnp
import numpy as np
from jax import lax
from jax.experimental import pallas as pl
from jax.experimental.pallas import tpu as pltpu
from jax.sharding import PartitionSpec as P

CHANNEL_COUNT = 192
PIX = 256
REACH = 3
WIDE = 24
PAD_ROWS = 544
SHIFT_ROWS = 528

EPSILON = 1e-06
GELU_SCALE = 0.7978845608
GELU_CUBIC = 0.044715

F32 = jnp.float32
BF16 = jnp.bfloat16
NT = (((1,), (1,)), ((), ()))


def placement():
    m = np.zeros((PAD_ROWS, 4 * PIX), np.float32)
    for i in range(22):
        for j in range(22):
            ii, jj = (i - 3) % 16, (j - 3) % 16
            inner_i, inner_j = 3 <= i < 19, 3 <= j < 19
            if inner_i and inner_j:
                part = 3
            elif inner_j:
                part = 0
            elif inner_i:
                part = 1
            else:
                part = 2
            m[i * WIDE + j, part * PIX + ii * 16 + jj] = 1.0
    return m


def fill_padded(ids, table, place, joined, pad):
    lane = lax.broadcasted_iota(jnp.int32, (48, PIX), 1)
    low = lane >= 128
    right = (lane % 16) >= 8

    def one(t, carry):
        def at(k):
            return table[ids[t, k]].astype(F32)

        rows = pl.ds(pl.multiple_of(t * 48, 48), 48)
        joined[rows, 0:PIX] = jnp.where(low, at(1), at(6)).astype(BF16)
        joined[rows, PIX : 2 * PIX] = jnp.where(right, at(3), at(4)).astype(BF16)
        joined[rows, 2 * PIX : 3 * PIX] = jnp.where(
            low, jnp.where(right, at(0), at(2)), jnp.where(right, at(5), at(7))
        ).astype(BF16)
        joined[rows, 3 * PIX : 4 * PIX] = table[REACH * 8 + t]
        return carry

    lax.fori_loop(0, 8, one, 0)
    pad[...] = lax.dot_general(place[...], joined[...], NT, preferred_element_type=F32)


def shift_copies(pad, shifted):
    for b in range(7):
        shifted[b] = pad[b : b + SHIFT_ROWS, :]


def convolve(shifted, weights, result):
    def row(i, carry):
        acc = jnp.zeros((16, 384), F32)
        for a in range(7):
            start = pl.multiple_of((i + a) * WIDE, 8)
            for b in range(7):
                tap = a * 7 + b
                acc = acc + weights[tap : tap + 1, :] * shifted[b, pl.ds(start, 16), :]
        result[pl.ds(pl.multiple_of(i * 16, 16), 16), :] = acc
        return carry

    lax.fori_loop(0, 16, row, 0)


def load_table(pieces, table):
    for o in range(7):
        table[o * 8 : o * 8 + 8] = pieces[o][...]
    table[56] = jnp.zeros((48, PIX), BF16)


def forward_conv(ids, p0, p1, p2, p3, p4, p5, p6, place, weights, mixed, padded,
                 table, joined, pad, shifted, result):
    load_table((p0, p1, p2, p3, p4, p5, p6), table)
    fill_padded(ids, table, place, joined, pad)
    padded[...] = pad[...].astype(BF16)
    shift_copies(pad, shifted)
    convolve(shifted, weights, result)
    mixed[...] = result[...].T.astype(BF16)


def backward_conv(ids, p0, p1, p2, p3, p4, p5, p6, place, weights, padded, cotangent, fold,
                  grad_in, grad_dw, table, joined, pad, shifted, result, taps):
    load_table((p0, p1, p2, p3, p4, p5, p6), table)
    fill_padded(ids, table, place, joined, pad)
    shift_copies(pad, shifted)
    convolve(shifted, weights, result)
    grad_in[...] = (cotangent[...].astype(F32) + result[...].T).astype(BF16)

    def keep(i, carry):
        start = pl.multiple_of((i + 3) * WIDE, 8)
        result[pl.ds(pl.multiple_of(i * 16, 16), 16), :] = shifted[3, pl.ds(start, 16), :]
        return carry

    lax.fori_loop(0, 16, keep, 0)
    pad[...] = padded[...].astype(F32)
    shift_copies(pad, shifted)
    for a in range(7):

        def row(i, sums):
            start = pl.multiple_of((i + a) * WIDE, 8)
            grad = result[pl.ds(pl.multiple_of(i * 16, 16), 16), :]
            new = []
            for b in range(7):
                prod = grad * shifted[b, pl.ds(start, 16), :]
                new.append(sums[b] + prod[0:8] + prod[8:16])
            return tuple(new)

        sums = lax.fori_loop(0, 16, row, tuple(jnp.zeros((8, 384), F32) for _ in range(7)))
        for b in range(7):
            tap = a * 7 + b
            taps[tap : tap + 1, :] = jnp.sum(sums[b], axis=0, keepdims=True)
    taps[49:56, :] = jnp.zeros((7, 384), F32)
    grad_dw[...] = jnp.dot(
        taps[...], fold[...], precision=lax.Precision.HIGHEST, preferred_element_type=F32
    )


def mlp(perm, m0, m1, m2, m3, d0, d1, d2, d3, wi, wit, wo, wot, bias,
        part_out, part_in, raw, stats, sum1, sum2):
    ms, ds = (m0, m1, m2, m3), (d0, d1, d2, d3)
    gain = jnp.concatenate([d[8].astype(F32) for d in ds], axis=0)
    sum1[...] = jnp.zeros_like(sum1)
    sum2[...] = jnp.zeros_like(sum2)
    for k in range(4):
        part_in[k, 8] = jnp.zeros((48, PIX), BF16)
    s1_all, s2_all = [], []
    for t in range(8):
        mixed = jnp.concatenate([m[t].astype(F32) for m in ms], axis=0)
        mean = jnp.sum(mixed, axis=0, keepdims=True) * (1.0 / CHANNEL_COUNT)
        square = jnp.sum(mixed * mixed, axis=0, keepdims=True) * (1.0 / CHANNEL_COUNT)
        inv = lax.rsqrt(square - mean * mean + EPSILON)
        xhat = (mixed - mean) * inv
        stats[0, t : t + 1, :] = mean
        stats[1, t : t + 1, :] = inv
        normed = (xhat * gain).astype(BF16)
        dbranch = jnp.concatenate([d[t] for d in ds], axis=0)
        pre = jnp.dot(wit[...], normed, preferred_element_type=F32) + bias[...]
        tangent = jnp.tanh(GELU_SCALE * (pre + GELU_CUBIC * pre * pre * pre))
        act = (0.5 * pre * (1.0 + tangent)).astype(BF16)
        slope = 0.5 * (1.0 + tangent) + 0.5 * pre * (1.0 - tangent * tangent) * GELU_SCALE * (
            1.0 + 3.0 * GELU_CUBIC * pre * pre
        )
        out = jnp.dot(wot[...], act, preferred_element_type=F32).astype(BF16)
        act_grad = jnp.dot(wo[...], dbranch, preferred_element_type=F32)
        pre_grad = (act_grad * slope).astype(BF16)
        back = jnp.dot(wi[...], pre_grad, preferred_element_type=F32).astype(BF16)
        sum1[...] += lax.dot_general(normed, pre_grad, NT, preferred_element_type=F32)
        sum2[...] += lax.dot_general(dbranch, act, NT, preferred_element_type=F32)
        for k in range(4):
            part_out[k, t] = out[k * 48 : k * 48 + 48]
            part_in[k, t] = back[k * 48 : k * 48 + 48]
        xgrad = back.astype(F32) * gain
        s1_all.append(jnp.sum(xgrad, axis=0, keepdims=True))
        s2_all.append(jnp.sum(xgrad * xhat, axis=0, keepdims=True))
    rows = []
    for total in (jnp.concatenate(s1_all, axis=0), jnp.concatenate(s2_all, axis=0)):
        high = total.astype(BF16).astype(F32)
        rows.append(high)
        rows.append(total - high)
    packed = jnp.concatenate(rows, axis=0).astype(BF16)
    for k in range(4):
        part_in[k, 8, 0:32, :] = packed
        raw[perm[k]] = sum1[k * 48 : k * 48 + 48, :].astype(BF16)
        raw[4 + perm[k]] = sum2[k * 48 : k * 48 + 48, :].astype(BF16)


VM = pl.BlockSpec(memory_space=pltpu.VMEM)
SM = pl.BlockSpec(memory_space=pltpu.SMEM)
PARAMS = pltpu.CompilerParams(vmem_limit_bytes=40 * 1024 * 1024)


def conv_scratch():
    return [
        pltpu.VMEM((57, 48, PIX), BF16),
        pltpu.VMEM((384, 4 * PIX), BF16),
        pltpu.VMEM((PAD_ROWS, 384), F32),
        pltpu.VMEM((7, SHIFT_ROWS, 384), F32),
        pltpu.VMEM((PIX, 384), F32),
    ]


def xor_pass(value, axis, bit):
    return lax.ppermute(value, axis, [(i, i ^ bit) for i in range(lax.axis_size(axis))])


def passed_along(value, axis, by):
    length = lax.axis_size(axis)
    pairs = [(i, i + by) for i in range(length) if 0 <= i + by < length]
    return lax.ppermute(value, axis, pairs)


def around(tiles):
    return [
        tiles if offset == 0 else passed_along(tiles, "tiles", -offset)
        for offset in range(-REACH, REACH + 1)
    ]


def relay_tiles(x_scan, slot_owner, tile_count):
    my_index = lax.axis_index("tiles")
    partner = jnp.bitwise_xor(my_index, 1)
    owner_dev = slot_owner // tile_count
    position = slot_owner % tile_count
    slots = jnp.arange(x_scan.shape[0], dtype=jnp.int32)
    targets = jnp.arange(tile_count, dtype=jnp.int32)
    half = tile_count // 2
    leaving = owner_dev == partner
    rank = jnp.cumsum(leaving.astype(jnp.int32)) - 1
    outgoing = (rank[None, :] == targets[:half, None]) & leaving[None, :]
    pick = jnp.sum(jnp.where(outgoing, slots[None, :], 0), axis=1)
    place = jnp.where(
        jnp.any(outgoing, axis=1),
        jnp.sum(jnp.where(outgoing, position[None, :], 0), axis=1),
        tile_count,
    )
    sent = jnp.take(x_scan, pick, axis=0, mode="clip")
    arrived, arrived_place = xor_pass((sent, place), "tiles", 1)
    staying = (position[None, :] == targets[:, None]) & (owner_dev == my_index)[None, :]
    source = jnp.sum(jnp.where(staying, slots[None, :], 0), axis=1)
    landed = arrived_place[None, :] == targets[:, None]
    ranks = targets[:half]
    source = source + jnp.sum(
        jnp.where(landed, x_scan.shape[0] + ranks[None, :], 0), axis=1
    )
    return jnp.take(jnp.concatenate([x_scan, arrived], axis=0), source, axis=0, mode="clip")


def body(
    x_scan, slot_owner, adjacency, cotangent, dw_weight, ln_gain, w_in, b_in, w_out, layer_scale
):
    tile_count = adjacency.shape[0]
    n_tiles = lax.axis_size("tiles")
    channels = x_scan.shape[1]
    rows = tile_count * channels
    me_t, me_c = lax.axis_index("tiles"), lax.axis_index("chan")
    scale_col = layer_scale[None, :, None]
    gain_float = ln_gain.astype(F32)[None, :, None]

    dbranch = (cotangent.astype(F32) * scale_col).astype(BF16)
    ext = jnp.concatenate(
        [dbranch, jnp.broadcast_to(ln_gain[None, :, None], (1, channels, PIX))], axis=0
    )
    d_all = [ext] + [xor_pass(ext, "chan", k) for k in (1, 2, 3)]

    perm = jnp.bitwise_xor(jnp.arange(4, dtype=jnp.int32), me_c)
    wi = jnp.take(w_in.reshape(4, channels, -1), perm, axis=0, mode="clip").reshape(w_in.shape)
    wot = jnp.take(w_out.T.reshape(4, channels, -1), perm, axis=0, mode="clip")
    wot = wot.reshape(CHANNEL_COUNT, -1)
    taps = jnp.tile(dw_weight.T, (1, tile_count))
    taps_back = jnp.tile(dw_weight[:, ::-1].T, (1, tile_count))
    place = jnp.asarray(placement(), BF16)
    fold = jnp.asarray(np.tile(np.eye(channels, dtype=np.float32), (tile_count, 1)))
    local_ids = adjacency - (me_t - REACH) * tile_count
    valid = (
        (adjacency < tile_count * n_tiles)
        & (local_ids >= 0)
        & (local_ids < (2 * REACH + 1) * tile_count)
    )
    ids = jnp.where(valid, local_ids, (2 * REACH + 1) * tile_count)

    owned = relay_tiles(x_scan, slot_owner, tile_count)
    mixed, padded = pl.pallas_call(
        forward_conv,
        out_shape=(
            jax.ShapeDtypeStruct((rows, PIX), BF16),
            jax.ShapeDtypeStruct((PAD_ROWS, rows), BF16),
        ),
        in_specs=[SM] + [VM] * 9,
        out_specs=(VM, VM),
        scratch_shapes=conv_scratch(),
        compiler_params=PARAMS,
        name="forward_conv",
    )(ids, *around(owned), place, taps)
    mixed = mixed.reshape(tile_count, channels, PIX)
    m_all = [mixed] + [xor_pass(mixed, "chan", k) for k in (1, 2, 3)]

    hidden = w_in.shape[1]
    part_out, part_in, raw, stats = pl.pallas_call(
        mlp,
        out_shape=(
            jax.ShapeDtypeStruct((4, tile_count, channels, PIX), BF16),
            jax.ShapeDtypeStruct((4, tile_count + 1, channels, PIX), BF16),
            jax.ShapeDtypeStruct((8, channels, hidden), BF16),
            jax.ShapeDtypeStruct((2, tile_count, PIX), F32),
        ),
        in_specs=[SM] + [VM] * 13,
        out_specs=(VM,) * 4,
        scratch_shapes=[pltpu.VMEM((CHANNEL_COUNT, hidden), F32)] * 2,
        compiler_params=PARAMS,
        name="mlp",
    )(perm, *m_all, *d_all, wi, wi.T, wot.T, wot, b_in.astype(F32)[:, None])

    back = [part_in[0]] + [xor_pass(part_in[k], "chan", k) for k in (1, 2, 3)]
    total = sum(b.astype(F32) for b in back[1:]) + back[0].astype(F32)
    dnormed = total[:tile_count]
    extra = total[tile_count]
    grad_sum = (extra[0:8] + extra[8:16]) / CHANNEL_COUNT
    grad_dot = (extra[16:24] + extra[24:32]) / CHANNEL_COUNT
    inv = stats[1][:, None, :]
    xhat = (mixed.astype(F32) - stats[0][:, None, :]) * inv
    dmixed = (
        inv * (dnormed * gain_float - grad_sum[:, None, :] - xhat * grad_dot[:, None, :])
    ).astype(BF16)

    pieces = around(dmixed)

    fwd = [part_out[0]] + [xor_pass(part_out[k], "chan", k) for k in (1, 2, 3)]
    branch = sum(b.astype(F32) for b in fwd[1:]) + fwd[0].astype(F32)
    branch = branch.astype(BF16).astype(F32)
    output = (owned.astype(F32) + scale_col * branch).astype(BF16)

    weights_sum = raw
    steps = [1 << s for s in range(n_tiles.bit_length() - 1)]
    for bit in steps:
        other = xor_pass(weights_sum, "tiles", bit)
        exact = weights_sum.astype(F32) + other.astype(F32)
        if bit != steps[-1]:
            exact = lax.reduce_precision(exact, 8, 7)
            weights_sum = exact.astype(BF16)
    factor = 1.0 / math.sqrt(tile_count * n_tiles * PIX)
    grad_w1 = exact[:4].reshape(CHANNEL_COUNT, hidden) * factor
    grad_w2 = (exact[4:].reshape(CHANNEL_COUNT, hidden) * factor).T

    grad_in, grad_dw = pl.pallas_call(
        backward_conv,
        out_shape=(
            jax.ShapeDtypeStruct((rows, PIX), BF16),
            jax.ShapeDtypeStruct((56, channels), F32),
        ),
        in_specs=[SM] + [VM] * 12,
        out_specs=(VM, VM),
        scratch_shapes=conv_scratch() + [pltpu.VMEM((56, rows), F32)],
        compiler_params=PARAMS,
        name="backward_conv",
    )(ids, *pieces, place, taps_back, padded, cotangent.reshape(rows, PIX), fold)
    for bit in steps:
        grad_dw = grad_dw + xor_pass(grad_dw, "tiles", bit)
    grad_dw = grad_dw[:49].T * factor
    return (output, grad_in.reshape(tile_count, channels, PIX), grad_dw, grad_w1, grad_w2)


def solution(mesh):
    in_specs = (
        P("tiles", "chan", None),
        P("tiles"),
        P("tiles", None),
        P("tiles", "chan", None),
        P("chan", None),
        P("chan"),
        P(None, "chan"),
        P("chan"),
        P("chan", None),
        P("chan"),
    )
    out_specs = (
        P("tiles", "chan", None),
        P("tiles", "chan", None),
        P("chan", None),
        P(None, "chan"),
        P("chan", None),
    )
    return jax.shard_map(body, mesh=mesh, in_specs=in_specs, out_specs=out_specs, check_vma=False)
```

```python
import functools
import math

import jax
import jax.numpy as jnp
import numpy as np
from jax import lax
from jax.experimental import pallas as pl
from jax.experimental.pallas import tpu as pltpu
from jax.sharding import PartitionSpec as P

CHANNEL_COUNT = 192
PIX = 256
REACH = 3
WIDE = 24
PAD_ROWS = 544
SHIFT_ROWS = 528

EPSILON = 1e-06
GELU_SCALE = 0.7978845608
GELU_CUBIC = 0.044715

F32 = jnp.float32
BF16 = jnp.bfloat16
NT = (((1,), (1,)), ((), ()))


def placement():
    m = np.zeros((PAD_ROWS, 4 * PIX), np.float32)
    for i in range(22):
        for j in range(22):
            ii, jj = (i - 3) % 16, (j - 3) % 16
            inner_i, inner_j = 3 <= i < 19, 3 <= j < 19
            if inner_i and inner_j:
                part = 3
            elif inner_j:
                part = 0
            elif inner_i:
                part = 1
            else:
                part = 2
            m[i * WIDE + j, part * PIX + ii * 16 + jj] = 1.0
    return m


def fill_padded(ids, table, place, joined, pad):
    lane = lax.broadcasted_iota(jnp.int32, (48, PIX), 1)
    low = lane >= 128
    right = (lane % 16) >= 8

    def one(t, carry):
        def at(k):
            return table[ids[t, k]].astype(F32)

        rows = pl.ds(pl.multiple_of(t * 48, 48), 48)
        joined[rows, 0:PIX] = jnp.where(low, at(1), at(6)).astype(BF16)
        joined[rows, PIX : 2 * PIX] = jnp.where(right, at(3), at(4)).astype(BF16)
        joined[rows, 2 * PIX : 3 * PIX] = jnp.where(
            low, jnp.where(right, at(0), at(2)), jnp.where(right, at(5), at(7))
        ).astype(BF16)
        joined[rows, 3 * PIX : 4 * PIX] = table[REACH * 8 + t]
        return carry

    lax.fori_loop(0, 8, one, 0)
    pad[...] = lax.dot_general(place[...], joined[...], NT, preferred_element_type=F32)


def shift_copies(pad, shifted):
    for b in range(7):
        shifted[b] = pad[b : b + SHIFT_ROWS, :]


def convolve(shifted, weights, result):
    def row(i, carry):
        acc = jnp.zeros((16, 384), F32)
        for a in range(7):
            start = pl.multiple_of((i + a) * WIDE, 8)
            for b in range(7):
                tap = a * 7 + b
                acc = acc + weights[tap : tap + 1, :] * shifted[b, pl.ds(start, 16), :]
        result[pl.ds(pl.multiple_of(i * 16, 16), 16), :] = acc
        return carry

    lax.fori_loop(0, 16, row, 0)


def load_table(pieces, table):
    table[0:56] = pieces[...]
    table[56] = jnp.zeros((48, PIX), BF16)


def exchange(length, own, table, local_sem, send_sems, recv_sems):
    me = lax.axis_index("tiles")
    barrier = pltpu.get_barrier_semaphore()
    offsets = [d for d in (3, -3, 2, -2, 1, -1) if abs(d) < length]

    def each(action):
        for d in offsets:
            inside = (me + d >= 0) & (me + d < length)
            pl.when(inside)(lambda d=d: action(d))

    def greet(d):
        pl.semaphore_signal(
            barrier, inc=1, device_id={"tiles": me + d}, device_id_type=pl.DeviceIdType.MESH
        )

    def copy(d):
        slot = REACH - d
        return pltpu.make_async_remote_copy(
            src_ref=own,
            dst_ref=table.at[pl.ds(slot * 8, 8)],
            send_sem=send_sems.at[slot],
            recv_sem=recv_sems.at[slot],
            device_id={"tiles": me + d},
            device_id_type=pl.DeviceIdType.MESH,
        )

    def arrival(d):
        slot = REACH + d
        return pltpu.make_async_remote_copy(
            src_ref=own,
            dst_ref=table.at[pl.ds(slot * 8, 8)],
            send_sem=send_sems.at[slot],
            recv_sem=recv_sems.at[slot],
            device_id={"tiles": me + d},
            device_id_type=pl.DeviceIdType.MESH,
        )

    each(greet)
    mine = pltpu.make_async_copy(own, table.at[pl.ds(REACH * 8, 8)], local_sem)
    mine.start()
    peers = jnp.minimum(me, REACH) + jnp.minimum(length - 1 - me, REACH)
    pl.semaphore_wait(barrier, peers)
    each(lambda d: copy(d).start())
    mine.wait()
    each(lambda d: copy(d).wait_send())
    each(lambda d: arrival(d).wait_recv())


def forward_conv(ids, pieces, place, weights, mixed, padded,
                 table, joined, pad, shifted, result):
    load_table(pieces, table)
    fill_padded(ids, table, place, joined, pad)
    padded[...] = pad[...].astype(BF16)
    shift_copies(pad, shifted)
    convolve(shifted, weights, result)
    mixed[...] = result[...].T.astype(BF16)


def backward_conv(ids, pieces, place, weights, cotangent,
                  grad_in, table, joined, pad, shifted, result):
    load_table(pieces, table)
    fill_padded(ids, table, place, joined, pad)
    shift_copies(pad, shifted)
    convolve(shifted, weights, result)
    grad_in[...] = (cotangent[...].astype(F32) + result[...].T).astype(BF16)


def kernel_grad(dmixed, padded, fold, grad_dw, pad, shifted, result, taps):
    result[...] = dmixed[...].astype(F32).T
    pad[...] = padded[...].astype(F32)
    shift_copies(pad, shifted)
    for a in range(7):

        def row(i, sums):
            start = pl.multiple_of((i + a) * WIDE, 8)
            grad = result[pl.ds(pl.multiple_of(i * 16, 16), 16), :]
            new = []
            for b in range(7):
                prod = grad * shifted[b, pl.ds(start, 16), :]
                new.append(sums[b] + prod[0:8] + prod[8:16])
            return tuple(new)

        sums = lax.fori_loop(0, 16, row, tuple(jnp.zeros((8, 384), F32) for _ in range(7)))
        for b in range(7):
            tap = a * 7 + b
            taps[tap : tap + 1, :] = jnp.sum(sums[b], axis=0, keepdims=True)
    taps[49:56, :] = jnp.zeros((7, 384), F32)
    grad_dw[...] = jnp.dot(
        taps[...], fold[...], precision=lax.Precision.HIGHEST, preferred_element_type=F32
    )


def mlp(perm, m0, m1, m2, m3, d0, d1, d2, d3, wi, wit, wo, wot, bias,
        part_out, part_in, raw, stats, sum1, sum2):
    ms, ds = (m0, m1, m2, m3), (d0, d1, d2, d3)
    gain = jnp.concatenate([d[8].astype(F32) for d in ds], axis=0)
    sum1[...] = jnp.zeros_like(sum1)
    sum2[...] = jnp.zeros_like(sum2)
    for k in range(4):
        part_in[k, 8] = jnp.zeros((48, PIX), BF16)
    s1_all, s2_all = [], []
    for t in range(8):
        mixed = jnp.concatenate([m[t].astype(F32) for m in ms], axis=0)
        mean = jnp.sum(mixed, axis=0, keepdims=True) * (1.0 / CHANNEL_COUNT)
        square = jnp.sum(mixed * mixed, axis=0, keepdims=True) * (1.0 / CHANNEL_COUNT)
        inv = lax.rsqrt(square - mean * mean + EPSILON)
        xhat = (mixed - mean) * inv
        stats[0, t : t + 1, :] = mean
        stats[1, t : t + 1, :] = inv
        normed = (xhat * gain).astype(BF16)
        dbranch = jnp.concatenate([d[t] for d in ds], axis=0)
        pre = jnp.dot(wit[...], normed, preferred_element_type=F32) + bias[...]
        tangent = jnp.tanh(GELU_SCALE * (pre + GELU_CUBIC * pre * pre * pre))
        act = (0.5 * pre * (1.0 + tangent)).astype(BF16)
        slope = 0.5 * (1.0 + tangent) + 0.5 * pre * (1.0 - tangent * tangent) * GELU_SCALE * (
            1.0 + 3.0 * GELU_CUBIC * pre * pre
        )
        out = jnp.dot(wot[...], act, preferred_element_type=F32).astype(BF16)
        act_grad = jnp.dot(wo[...], dbranch, preferred_element_type=F32)
        pre_grad = (act_grad * slope).astype(BF16)
        back = jnp.dot(wi[...], pre_grad, preferred_element_type=F32).astype(BF16)
        sum1[...] += lax.dot_general(normed, pre_grad, NT, preferred_element_type=F32)
        sum2[...] += lax.dot_general(dbranch, act, NT, preferred_element_type=F32)
        for k in range(4):
            part_out[k, t] = out[k * 48 : k * 48 + 48]
            part_in[k, t] = back[k * 48 : k * 48 + 48]
        xgrad = back.astype(F32) * gain
        s1_all.append(jnp.sum(xgrad, axis=0, keepdims=True))
        s2_all.append(jnp.sum(xgrad * xhat, axis=0, keepdims=True))
    rows = []
    for total in (jnp.concatenate(s1_all, axis=0), jnp.concatenate(s2_all, axis=0)):
        high = total.astype(BF16).astype(F32)
        rows.append(high)
        rows.append(total - high)
    packed = jnp.concatenate(rows, axis=0).astype(BF16)
    for k in range(4):
        part_in[k, 8, 0:32, :] = packed
        raw[perm[k]] = sum1[k * 48 : k * 48 + 48, :].astype(BF16)
        raw[4 + perm[k]] = sum2[k * 48 : k * 48 + 48, :].astype(BF16)


VM = pl.BlockSpec(memory_space=pltpu.VMEM)
SM = pl.BlockSpec(memory_space=pltpu.SMEM)
PARAMS = pltpu.CompilerParams(vmem_limit_bytes=40 * 1024 * 1024)


def conv_scratch():
    return [
        pltpu.VMEM((57, 48, PIX), BF16),
        pltpu.VMEM((384, 4 * PIX), BF16),
        pltpu.VMEM((PAD_ROWS, 384), F32),
        pltpu.VMEM((7, SHIFT_ROWS, 384), F32),
        pltpu.VMEM((PIX, 384), F32),
    ]


def xor_pass(value, axis, bit):
    return lax.ppermute(value, axis, [(i, i ^ bit) for i in range(lax.axis_size(axis))])


def around(tiles, n_tiles, collective_id):
    count, channels, pix = tiles.shape
    anywhere = pl.BlockSpec(memory_space=pl.ANY)
    return pl.pallas_call(
        functools.partial(exchange, n_tiles),
        out_shape=jax.ShapeDtypeStruct(((2 * REACH + 1) * count, channels, pix), tiles.dtype),
        in_specs=[anywhere],
        out_specs=anywhere,
        scratch_shapes=[
            pltpu.SemaphoreType.DMA,
            pltpu.SemaphoreType.DMA((2 * REACH + 1,)),
            pltpu.SemaphoreType.DMA((2 * REACH + 1,)),
        ],
        compiler_params=pltpu.CompilerParams(
            collective_id=collective_id, has_side_effects=True
        ),
        cost_estimate=pl.CostEstimate(flops=0, bytes_accessed=40_000_000, transcendentals=0),
        name="exchange",
    )(tiles)


def relay_tiles(x_scan, slot_owner, tile_count):
    my_index = lax.axis_index("tiles")
    partner = jnp.bitwise_xor(my_index, 1)
    owner_dev = slot_owner // tile_count
    position = slot_owner % tile_count
    slots = jnp.arange(x_scan.shape[0], dtype=jnp.int32)
    targets = jnp.arange(tile_count, dtype=jnp.int32)
    half = tile_count // 2
    leaving = owner_dev == partner
    rank = jnp.cumsum(leaving.astype(jnp.int32)) - 1
    outgoing = (rank[None, :] == targets[:half, None]) & leaving[None, :]
    pick = jnp.sum(jnp.where(outgoing, slots[None, :], 0), axis=1)
    place = jnp.where(
        jnp.any(outgoing, axis=1),
        jnp.sum(jnp.where(outgoing, position[None, :], 0), axis=1),
        tile_count,
    )
    sent = jnp.take(x_scan, pick, axis=0, mode="clip")
    arrived, arrived_place = xor_pass((sent, place), "tiles", 1)
    staying = (position[None, :] == targets[:, None]) & (owner_dev == my_index)[None, :]
    source = jnp.sum(jnp.where(staying, slots[None, :], 0), axis=1)
    landed = arrived_place[None, :] == targets[:, None]
    ranks = targets[:half]
    source = source + jnp.sum(
        jnp.where(landed, x_scan.shape[0] + ranks[None, :], 0), axis=1
    )
    return jnp.take(jnp.concatenate([x_scan, arrived], axis=0), source, axis=0, mode="clip")


def body(
    x_scan, slot_owner, adjacency, cotangent, dw_weight, ln_gain, w_in, b_in, w_out, layer_scale
):
    tile_count = adjacency.shape[0]
    n_tiles = lax.axis_size("tiles")
    channels = x_scan.shape[1]
    rows = tile_count * channels
    me_t, me_c = lax.axis_index("tiles"), lax.axis_index("chan")
    scale_col = layer_scale[None, :, None]
    gain_float = ln_gain.astype(F32)[None, :, None]

    dbranch = (cotangent.astype(F32) * scale_col).astype(BF16)
    ext = jnp.concatenate(
        [dbranch, jnp.broadcast_to(ln_gain[None, :, None], (1, channels, PIX))], axis=0
    )
    d_all = [ext] + [xor_pass(ext, "chan", k) for k in (1, 2, 3)]

    perm = jnp.bitwise_xor(jnp.arange(4, dtype=jnp.int32), me_c)
    wi = jnp.take(w_in.reshape(4, channels, -1), perm, axis=0, mode="clip").reshape(w_in.shape)
    wot = jnp.take(w_out.T.reshape(4, channels, -1), perm, axis=0, mode="clip")
    wot = wot.reshape(CHANNEL_COUNT, -1)
    taps = jnp.tile(dw_weight.T, (1, tile_count))
    taps_back = jnp.tile(dw_weight[:, ::-1].T, (1, tile_count))
    place = jnp.asarray(placement(), BF16)
    fold = jnp.asarray(np.tile(np.eye(channels, dtype=np.float32), (tile_count, 1)))
    local_ids = adjacency - (me_t - REACH) * tile_count
    valid = (
        (adjacency < tile_count * n_tiles)
        & (local_ids >= 0)
        & (local_ids < (2 * REACH + 1) * tile_count)
    )
    ids = jnp.where(valid, local_ids, (2 * REACH + 1) * tile_count)

    owned = relay_tiles(x_scan, slot_owner, tile_count)
    mixed, padded = pl.pallas_call(
        forward_conv,
        out_shape=(
            jax.ShapeDtypeStruct((rows, PIX), BF16),
            jax.ShapeDtypeStruct((PAD_ROWS, rows), BF16),
        ),
        in_specs=[SM] + [VM] * 3,
        out_specs=(VM, VM),
        scratch_shapes=conv_scratch(),
        compiler_params=PARAMS,
        name="forward_conv",
    )(ids, around(owned, n_tiles, 0), place, taps)
    mixed = mixed.reshape(tile_count, channels, PIX)
    m_all = [mixed] + [xor_pass(mixed, "chan", k) for k in (1, 2, 3)]

    hidden = w_in.shape[1]
    part_out, part_in, raw, stats = pl.pallas_call(
        mlp,
        out_shape=(
            jax.ShapeDtypeStruct((4, tile_count, channels, PIX), BF16),
            jax.ShapeDtypeStruct((4, tile_count + 1, channels, PIX), BF16),
            jax.ShapeDtypeStruct((8, channels, hidden), BF16),
            jax.ShapeDtypeStruct((2, tile_count, PIX), F32),
        ),
        in_specs=[SM] + [VM] * 13,
        out_specs=(VM,) * 4,
        scratch_shapes=[pltpu.VMEM((CHANNEL_COUNT, hidden), F32)] * 2,
        compiler_params=PARAMS,
        name="mlp",
    )(perm, *m_all, *d_all, wi, wi.T, wot.T, wot, b_in.astype(F32)[:, None])

    back = [part_in[0]] + [xor_pass(part_in[k], "chan", k) for k in (1, 2, 3)]
    total = sum(b.astype(F32) for b in back[1:]) + back[0].astype(F32)
    dnormed = total[:tile_count]
    extra = total[tile_count]
    grad_sum = (extra[0:8] + extra[8:16]) / CHANNEL_COUNT
    grad_dot = (extra[16:24] + extra[24:32]) / CHANNEL_COUNT
    inv = stats[1][:, None, :]
    xhat = (mixed.astype(F32) - stats[0][:, None, :]) * inv
    dmixed = (
        inv * (dnormed * gain_float - grad_sum[:, None, :] - xhat * grad_dot[:, None, :])
    ).astype(BF16)

    steps = [1 << s for s in range(n_tiles.bit_length() - 1)]
    grad_dw = pl.pallas_call(
        kernel_grad,
        out_shape=jax.ShapeDtypeStruct((56, channels), F32),
        in_specs=[VM] * 3,
        out_specs=VM,
        scratch_shapes=conv_scratch()[2:] + [pltpu.VMEM((56, rows), F32)],
        compiler_params=PARAMS,
        name="kernel_grad",
    )(dmixed.reshape(rows, PIX), padded, fold)
    for bit in steps:
        grad_dw = grad_dw + xor_pass(grad_dw, "tiles", bit)
    pieces = around(dmixed, n_tiles, 1)

    fwd = [part_out[0]] + [xor_pass(part_out[k], "chan", k) for k in (1, 2, 3)]
    branch = sum(b.astype(F32) for b in fwd[1:]) + fwd[0].astype(F32)
    branch = branch.astype(BF16).astype(F32)
    output = (owned.astype(F32) + scale_col * branch).astype(BF16)

    weights_sum = raw
    for bit in steps:
        other = xor_pass(weights_sum, "tiles", bit)
        exact = weights_sum.astype(F32) + other.astype(F32)
        if bit != steps[-1]:
            exact = lax.reduce_precision(exact, 8, 7)
            weights_sum = exact.astype(BF16)
    factor = 1.0 / math.sqrt(tile_count * n_tiles * PIX)
    grad_w1 = exact[:4].reshape(CHANNEL_COUNT, hidden) * factor
    grad_w2 = (exact[4:].reshape(CHANNEL_COUNT, hidden) * factor).T

    grad_in = pl.pallas_call(
        backward_conv,
        out_shape=jax.ShapeDtypeStruct((rows, PIX), BF16),
        in_specs=[SM] + [VM] * 4,
        out_specs=VM,
        scratch_shapes=conv_scratch(),
        compiler_params=PARAMS,
        name="backward_conv",
    )(ids, pieces, place, taps_back, cotangent.reshape(rows, PIX))
    grad_dw = grad_dw[:49].T * factor
    return (output, grad_in.reshape(tile_count, channels, PIX), grad_dw, grad_w1, grad_w2)


def solution(mesh):
    in_specs = (
        P("tiles", "chan", None),
        P("tiles"),
        P("tiles", None),
        P("tiles", "chan", None),
        P("chan", None),
        P("chan"),
        P(None, "chan"),
        P("chan"),
        P("chan", None),
        P("chan"),
    )
    out_specs = (
        P("tiles", "chan", None),
        P("tiles", "chan", None),
        P("chan", None),
        P(None, "chan"),
        P("chan", None),
    )
    return jax.shard_map(body, mesh=mesh, in_specs=in_specs, out_specs=out_specs, check_vma=False)
```

```python
import functools
import math

import jax
import jax.numpy as jnp
import numpy as np
from jax import lax
from jax.experimental import pallas as pl
from jax.experimental.pallas import tpu as pltpu
from jax.sharding import PartitionSpec as P

CHANNEL_COUNT = 192
PIX = 256
REACH = 3
WIDE = 24
PAD_ROWS = 544
SHIFT_ROWS = 528

EPSILON = 1e-06
GELU_SCALE = 0.7978845608
GELU_CUBIC = 0.044715

F32 = jnp.float32
BF16 = jnp.bfloat16
NT = (((1,), (1,)), ((), ()))


def placement():
    m = np.zeros((PAD_ROWS, 4 * PIX), np.float32)
    for i in range(22):
        for j in range(22):
            ii, jj = (i - 3) % 16, (j - 3) % 16
            inner_i, inner_j = 3 <= i < 19, 3 <= j < 19
            if inner_i and inner_j:
                part = 3
            elif inner_j:
                part = 0
            elif inner_i:
                part = 1
            else:
                part = 2
            m[i * WIDE + j, part * PIX + ii * 16 + jj] = 1.0
    return m


def fill_padded(ids, table, place, joined, pad):
    lane = lax.broadcasted_iota(jnp.int32, (48, PIX), 1)
    low = lane >= 128
    right = (lane % 16) >= 8

    def one(t, carry):
        def at(k):
            return table[ids[t, k]].astype(F32)

        rows = pl.ds(pl.multiple_of(t * 48, 48), 48)
        joined[rows, 0:PIX] = jnp.where(low, at(1), at(6)).astype(BF16)
        joined[rows, PIX : 2 * PIX] = jnp.where(right, at(3), at(4)).astype(BF16)
        joined[rows, 2 * PIX : 3 * PIX] = jnp.where(
            low, jnp.where(right, at(0), at(2)), jnp.where(right, at(5), at(7))
        ).astype(BF16)
        joined[rows, 3 * PIX : 4 * PIX] = table[REACH * 8 + t]
        return carry

    lax.fori_loop(0, 8, one, 0)
    pad[...] = lax.dot_general(place[...], joined[...], NT, preferred_element_type=F32)


def shift_copies(pad, shifted):
    for b in range(7):
        shifted[b] = pad[b : b + SHIFT_ROWS, :]


def convolve(shifted, weights, result):
    def row(i, carry):
        acc = jnp.zeros((16, 384), F32)
        for a in range(7):
            start = pl.multiple_of((i + a) * WIDE, 8)
            for b in range(7):
                tap = a * 7 + b
                acc = acc + weights[tap : tap + 1, :] * shifted[b, pl.ds(start, 16), :]
        result[pl.ds(pl.multiple_of(i * 16, 16), 16), :] = acc
        return carry

    lax.fori_loop(0, 16, row, 0)


def load_table(pieces, table):
    table[0:56] = pieces[...]
    table[56] = jnp.zeros((48, PIX), BF16)


def exchange(length, own, table, local_sem, send_sems, recv_sems):
    me = lax.axis_index("tiles")
    barrier = pltpu.get_barrier_semaphore()
    offsets = [d for d in (3, -3, 2, -2, 1, -1) if abs(d) < length]

    def each(action):
        for d in offsets:
            inside = (me + d >= 0) & (me + d < length)
            pl.when(inside)(lambda d=d: action(d))

    def greet(d):
        pl.semaphore_signal(
            barrier, inc=1, device_id={"tiles": me + d}, device_id_type=pl.DeviceIdType.MESH
        )

    def used(slot):
        if slot >= REACH + 2:
            return pl.ds(0, PIX // 2)
        if slot <= REACH - 2:
            return pl.ds(PIX // 2, PIX // 2)
        return pl.ds(0, PIX)

    def copy(d):
        slot = REACH - d
        return pltpu.make_async_remote_copy(
            src_ref=own.at[:, :, used(slot)],
            dst_ref=table.at[pl.ds(slot * 8, 8), :, used(slot)],
            send_sem=send_sems.at[slot],
            recv_sem=recv_sems.at[slot],
            device_id={"tiles": me + d},
            device_id_type=pl.DeviceIdType.MESH,
        )

    def arrival(d):
        slot = REACH + d
        return pltpu.make_async_remote_copy(
            src_ref=own.at[:, :, used(slot)],
            dst_ref=table.at[pl.ds(slot * 8, 8), :, used(slot)],
            send_sem=send_sems.at[slot],
            recv_sem=recv_sems.at[slot],
            device_id={"tiles": me + d},
            device_id_type=pl.DeviceIdType.MESH,
        )

    each(greet)
    mine = pltpu.make_async_copy(own, table.at[pl.ds(REACH * 8, 8)], local_sem)
    mine.start()
    peers = jnp.minimum(me, REACH) + jnp.minimum(length - 1 - me, REACH)
    pl.semaphore_wait(barrier, peers)
    each(lambda d: copy(d).start())
    mine.wait()
    each(lambda d: copy(d).wait_send())
    each(lambda d: arrival(d).wait_recv())


def forward_conv(ids, pieces, place, weights, mixed, padded,
                 table, joined, pad, shifted, result):
    load_table(pieces, table)
    fill_padded(ids, table, place, joined, pad)
    padded[...] = pad[...].astype(BF16)
    shift_copies(pad, shifted)
    convolve(shifted, weights, result)
    mixed[...] = result[...].T.astype(BF16)


def backward_conv(ids, pieces, place, weights, cotangent,
                  grad_in, table, joined, pad, shifted, result):
    load_table(pieces, table)
    fill_padded(ids, table, place, joined, pad)
    shift_copies(pad, shifted)
    convolve(shifted, weights, result)
    grad_in[...] = (cotangent[...].astype(F32) + result[...].T).astype(BF16)


def kernel_grad(dmixed, padded, fold, grad_dw, pad, shifted, result, taps):
    result[...] = dmixed[...].astype(F32).T
    pad[...] = padded[...].astype(F32)
    shift_copies(pad, shifted)
    for a in range(7):

        def row(i, sums):
            start = pl.multiple_of((i + a) * WIDE, 8)
            grad = result[pl.ds(pl.multiple_of(i * 16, 16), 16), :]
            new = []
            for b in range(7):
                prod = grad * shifted[b, pl.ds(start, 16), :]
                new.append(sums[b] + prod[0:8] + prod[8:16])
            return tuple(new)

        sums = lax.fori_loop(0, 16, row, tuple(jnp.zeros((8, 384), F32) for _ in range(7)))
        for b in range(7):
            tap = a * 7 + b
            taps[tap : tap + 1, :] = jnp.sum(sums[b], axis=0, keepdims=True)
    taps[49:56, :] = jnp.zeros((7, 384), F32)
    grad_dw[...] = jnp.dot(
        taps[...], fold[...], precision=lax.Precision.HIGHEST, preferred_element_type=F32
    )


def mlp(perm, m0, m1, m2, m3, d0, d1, d2, d3, wi, wit, wo, wot, bias,
        part_out, part_in, raw, stats, sum1, sum2):
    ms, ds = (m0, m1, m2, m3), (d0, d1, d2, d3)
    gain = jnp.concatenate([d[8].astype(F32) for d in ds], axis=0)
    sum1[...] = jnp.zeros_like(sum1)
    sum2[...] = jnp.zeros_like(sum2)
    for k in range(4):
        part_in[k, 8] = jnp.zeros((48, PIX), BF16)
    s1_all, s2_all = [], []
    for t in range(8):
        mixed = jnp.concatenate([m[t].astype(F32) for m in ms], axis=0)
        mean = jnp.sum(mixed, axis=0, keepdims=True) * (1.0 / CHANNEL_COUNT)
        square = jnp.sum(mixed * mixed, axis=0, keepdims=True) * (1.0 / CHANNEL_COUNT)
        inv = lax.rsqrt(square - mean * mean + EPSILON)
        xhat = (mixed - mean) * inv
        stats[0, t : t + 1, :] = mean
        stats[1, t : t + 1, :] = inv
        normed = (xhat * gain).astype(BF16)
        dbranch = jnp.concatenate([d[t] for d in ds], axis=0)
        pre = jnp.dot(wit[...], normed, preferred_element_type=F32) + bias[...]
        tangent = jnp.tanh(GELU_SCALE * (pre + GELU_CUBIC * pre * pre * pre))
        act = (0.5 * pre * (1.0 + tangent)).astype(BF16)
        slope = 0.5 * (1.0 + tangent) + 0.5 * pre * (1.0 - tangent * tangent) * GELU_SCALE * (
            1.0 + 3.0 * GELU_CUBIC * pre * pre
        )
        out = jnp.dot(wot[...], act, preferred_element_type=F32).astype(BF16)
        act_grad = jnp.dot(wo[...], dbranch, preferred_element_type=F32)
        pre_grad = (act_grad * slope).astype(BF16)
        back = jnp.dot(wi[...], pre_grad, preferred_element_type=F32).astype(BF16)
        sum1[...] += lax.dot_general(normed, pre_grad, NT, preferred_element_type=F32)
        sum2[...] += lax.dot_general(dbranch, act, NT, preferred_element_type=F32)
        for k in range(4):
            part_out[k, t] = out[k * 48 : k * 48 + 48]
            part_in[k, t] = back[k * 48 : k * 48 + 48]
        xgrad = back.astype(F32) * gain
        s1_all.append(jnp.sum(xgrad, axis=0, keepdims=True))
        s2_all.append(jnp.sum(xgrad * xhat, axis=0, keepdims=True))
    rows = []
    for total in (jnp.concatenate(s1_all, axis=0), jnp.concatenate(s2_all, axis=0)):
        high = total.astype(BF16).astype(F32)
        rows.append(high)
        rows.append(total - high)
    packed = jnp.concatenate(rows, axis=0).astype(BF16)
    for k in range(4):
        part_in[k, 8, 0:32, :] = packed
        raw[perm[k]] = sum1[k * 48 : k * 48 + 48, :].astype(BF16)
        raw[4 + perm[k]] = sum2[k * 48 : k * 48 + 48, :].astype(BF16)


VM = pl.BlockSpec(memory_space=pltpu.VMEM)
SM = pl.BlockSpec(memory_space=pltpu.SMEM)
PARAMS = pltpu.CompilerParams(vmem_limit_bytes=40 * 1024 * 1024)


def conv_scratch():
    return [
        pltpu.VMEM((57, 48, PIX), BF16),
        pltpu.VMEM((384, 4 * PIX), BF16),
        pltpu.VMEM((PAD_ROWS, 384), F32),
        pltpu.VMEM((7, SHIFT_ROWS, 384), F32),
        pltpu.VMEM((PIX, 384), F32),
    ]


def xor_pass(value, axis, bit):
    return lax.ppermute(value, axis, [(i, i ^ bit) for i in range(lax.axis_size(axis))])


def around(tiles, n_tiles, collective_id):
    count, channels, pix = tiles.shape
    anywhere = pl.BlockSpec(memory_space=pl.ANY)
    return pl.pallas_call(
        functools.partial(exchange, n_tiles),
        out_shape=jax.ShapeDtypeStruct(((2 * REACH + 1) * count, channels, pix), tiles.dtype),
        in_specs=[anywhere],
        out_specs=anywhere,
        scratch_shapes=[
            pltpu.SemaphoreType.DMA,
            pltpu.SemaphoreType.DMA((2 * REACH + 1,)),
            pltpu.SemaphoreType.DMA((2 * REACH + 1,)),
        ],
        compiler_params=pltpu.CompilerParams(
            collective_id=collective_id, has_side_effects=True
        ),
        cost_estimate=pl.CostEstimate(flops=0, bytes_accessed=40_000_000, transcendentals=0),
        name="exchange",
    )(tiles)


def relay_tiles(x_scan, slot_owner, tile_count):
    my_index = lax.axis_index("tiles")
    partner = jnp.bitwise_xor(my_index, 1)
    owner_dev = slot_owner // tile_count
    position = slot_owner % tile_count
    slots = jnp.arange(x_scan.shape[0], dtype=jnp.int32)
    targets = jnp.arange(tile_count, dtype=jnp.int32)
    half = tile_count // 2
    leaving = owner_dev == partner
    rank = jnp.cumsum(leaving.astype(jnp.int32)) - 1
    outgoing = (rank[None, :] == targets[:half, None]) & leaving[None, :]
    pick = jnp.sum(jnp.where(outgoing, slots[None, :], 0), axis=1)
    place = jnp.where(
        jnp.any(outgoing, axis=1),
        jnp.sum(jnp.where(outgoing, position[None, :], 0), axis=1),
        tile_count,
    )
    sent = jnp.take(x_scan, pick, axis=0, mode="clip")
    arrived, arrived_place = xor_pass((sent, place), "tiles", 1)
    staying = (position[None, :] == targets[:, None]) & (owner_dev == my_index)[None, :]
    source = jnp.sum(jnp.where(staying, slots[None, :], 0), axis=1)
    landed = arrived_place[None, :] == targets[:, None]
    ranks = targets[:half]
    source = source + jnp.sum(
        jnp.where(landed, x_scan.shape[0] + ranks[None, :], 0), axis=1
    )
    return jnp.take(jnp.concatenate([x_scan, arrived], axis=0), source, axis=0, mode="clip")


def body(
    x_scan, slot_owner, adjacency, cotangent, dw_weight, ln_gain, w_in, b_in, w_out, layer_scale
):
    tile_count = adjacency.shape[0]
    n_tiles = lax.axis_size("tiles")
    channels = x_scan.shape[1]
    rows = tile_count * channels
    me_t, me_c = lax.axis_index("tiles"), lax.axis_index("chan")
    scale_col = layer_scale[None, :, None]
    gain_float = ln_gain.astype(F32)[None, :, None]

    dbranch = (cotangent.astype(F32) * scale_col).astype(BF16)
    ext = jnp.concatenate(
        [dbranch, jnp.broadcast_to(ln_gain[None, :, None], (1, channels, PIX))], axis=0
    )
    d_all = [ext] + [xor_pass(ext, "chan", k) for k in (1, 2, 3)]

    perm = jnp.bitwise_xor(jnp.arange(4, dtype=jnp.int32), me_c)
    wi = jnp.take(w_in.reshape(4, channels, -1), perm, axis=0, mode="clip").reshape(w_in.shape)
    wot = jnp.take(w_out.T.reshape(4, channels, -1), perm, axis=0, mode="clip")
    wot = wot.reshape(CHANNEL_COUNT, -1)
    taps = jnp.tile(dw_weight.T, (1, tile_count))
    taps_back = jnp.tile(dw_weight[:, ::-1].T, (1, tile_count))
    place = jnp.asarray(placement(), BF16)
    fold = jnp.asarray(np.tile(np.eye(channels, dtype=np.float32), (tile_count, 1)))
    local_ids = adjacency - (me_t - REACH) * tile_count
    valid = (
        (adjacency < tile_count * n_tiles)
        & (local_ids >= 0)
        & (local_ids < (2 * REACH + 1) * tile_count)
    )
    ids = jnp.where(valid, local_ids, (2 * REACH + 1) * tile_count)

    owned = relay_tiles(x_scan, slot_owner, tile_count)
    mixed, padded = pl.pallas_call(
        forward_conv,
        out_shape=(
            jax.ShapeDtypeStruct((rows, PIX), BF16),
            jax.ShapeDtypeStruct((PAD_ROWS, rows), BF16),
        ),
        in_specs=[SM] + [VM] * 3,
        out_specs=(VM, VM),
        scratch_shapes=conv_scratch(),
        compiler_params=PARAMS,
        name="forward_conv",
    )(ids, around(owned, n_tiles, 0), place, taps)
    mixed = mixed.reshape(tile_count, channels, PIX)
    m_all = [mixed] + [xor_pass(mixed, "chan", k) for k in (1, 2, 3)]

    hidden = w_in.shape[1]
    part_out, part_in, raw, stats = pl.pallas_call(
        mlp,
        out_shape=(
            jax.ShapeDtypeStruct((4, tile_count, channels, PIX), BF16),
            jax.ShapeDtypeStruct((4, tile_count + 1, channels, PIX), BF16),
            jax.ShapeDtypeStruct((8, channels, hidden), BF16),
            jax.ShapeDtypeStruct((2, tile_count, PIX), F32),
        ),
        in_specs=[SM] + [VM] * 13,
        out_specs=(VM,) * 4,
        scratch_shapes=[pltpu.VMEM((CHANNEL_COUNT, hidden), F32)] * 2,
        compiler_params=PARAMS,
        name="mlp",
    )(perm, *m_all, *d_all, wi, wi.T, wot.T, wot, b_in.astype(F32)[:, None])

    back = [part_in[0]] + [xor_pass(part_in[k], "chan", k) for k in (1, 2, 3)]
    total = sum(b.astype(F32) for b in back[1:]) + back[0].astype(F32)
    dnormed = total[:tile_count]
    extra = total[tile_count]
    grad_sum = (extra[0:8] + extra[8:16]) / CHANNEL_COUNT
    grad_dot = (extra[16:24] + extra[24:32]) / CHANNEL_COUNT
    inv = stats[1][:, None, :]
    xhat = (mixed.astype(F32) - stats[0][:, None, :]) * inv
    dmixed = (
        inv * (dnormed * gain_float - grad_sum[:, None, :] - xhat * grad_dot[:, None, :])
    ).astype(BF16)

    steps = [1 << s for s in range(n_tiles.bit_length() - 1)]
    grad_dw = pl.pallas_call(
        kernel_grad,
        out_shape=jax.ShapeDtypeStruct((56, channels), F32),
        in_specs=[VM] * 3,
        out_specs=VM,
        scratch_shapes=conv_scratch()[2:] + [pltpu.VMEM((56, rows), F32)],
        compiler_params=PARAMS,
        name="kernel_grad",
    )(dmixed.reshape(rows, PIX), padded, fold)
    for bit in steps:
        grad_dw = grad_dw + xor_pass(grad_dw, "tiles", bit)
    pieces = around(dmixed, n_tiles, 1)

    fwd = [part_out[0]] + [xor_pass(part_out[k], "chan", k) for k in (1, 2, 3)]
    branch = sum(b.astype(F32) for b in fwd[1:]) + fwd[0].astype(F32)
    branch = branch.astype(BF16).astype(F32)
    output = (owned.astype(F32) + scale_col * branch).astype(BF16)

    weights_sum = raw
    for bit in steps:
        other = xor_pass(weights_sum, "tiles", bit)
        exact = weights_sum.astype(F32) + other.astype(F32)
        if bit != steps[-1]:
            exact = lax.reduce_precision(exact, 8, 7)
            weights_sum = exact.astype(BF16)
    factor = 1.0 / math.sqrt(tile_count * n_tiles * PIX)
    grad_w1 = exact[:4].reshape(CHANNEL_COUNT, hidden) * factor
    grad_w2 = (exact[4:].reshape(CHANNEL_COUNT, hidden) * factor).T

    grad_in = pl.pallas_call(
        backward_conv,
        out_shape=jax.ShapeDtypeStruct((rows, PIX), BF16),
        in_specs=[SM] + [VM] * 4,
        out_specs=VM,
        scratch_shapes=conv_scratch(),
        compiler_params=PARAMS,
        name="backward_conv",
    )(ids, pieces, place, taps_back, cotangent.reshape(rows, PIX))
    grad_dw = grad_dw[:49].T * factor
    return (output, grad_in.reshape(tile_count, channels, PIX), grad_dw, grad_w1, grad_w2)


def solution(mesh):
    in_specs = (
        P("tiles", "chan", None),
        P("tiles"),
        P("tiles", None),
        P("tiles", "chan", None),
        P("chan", None),
        P("chan"),
        P(None, "chan"),
        P("chan"),
        P("chan", None),
        P("chan"),
    )
    out_specs = (
        P("tiles", "chan", None),
        P("tiles", "chan", None),
        P("chan", None),
        P(None, "chan"),
        P("chan", None),
    )
    return jax.shard_map(body, mesh=mesh, in_specs=in_specs, out_specs=out_specs, check_vma=False)
```
